128 devices in a mesh: side: 2 (over core), gx: 64 (over z, x, y).
Axes of the slice: x: 4, y: 4, z: 4, core: 2. Of those that a mesh axis runs over, the one named last changes fastest.
Arguments:
- query: bfloat16 [1024, 8192], P(('side', 'gx')), may hold values from -18 to 18
- new_key: bfloat16 [1024, 1024], P(('side', 'gx')), may hold values from -6 to 6
- new_value: bfloat16 [1024, 1024], P(('side', 'gx')), may hold values from -6 to 6
- key_cache: bfloat16 [1024, 384, 1024], P(('side', 'gx')), may hold values from -18 to 18
- value_cache: bfloat16 [1024, 384, 1024], P(('side', 'gx')), may hold values from -6 to 6
- lengths: int32 [1024], P(('side', 'gx')), may hold values from 1 to 384, as said below
- residual: float32 [1024, 8192], P(('side', 'gx')), may hold values from -6 to 6
- norm_gain: float32 [8192], replicated, may hold values from 0.25 to 1.75
- gate_weight: bfloat16 [8192, 28672], P('side', 'gx'), may hold values from -0.0625 to 0.0625
- up_weight: bfloat16 [8192, 28672], P('side', 'gx'), may hold values from -0.0625 to 0.0625
- down_weight: bfloat16 [28672, 8192], P('gx', 'side'), may hold values from -0.03125 to 0.03125
Outputs:
- mixed: bfloat16 [1024, 8192], P(('side', 'gx'))
The draws below stay inside these ranges and needn't reach their ends.
Inputs may be any that keep to these rules, and one draw needn't show every extreme that they name: `lengths`: every request has at least one valid cached position; some request has all 384.
All inputs are finite; a program needn't handle non-finite values.
Results may differ from the reference program's by a relative error of at most 0.015.
Values may be sent and summed in bfloat16 or wider, within the bound.
No kernel may reach another device: no remote copies, remote signals or barrier semaphores. Data moves between devices by JAX's collectives and lax.ppermute only.
A program may use at most 128 MiB of HBM per device.

```python
import jax
import jax.numpy as jnp
from jax import lax

D = 8192
FF = 28672
HEADS = 64
KVH = 8
HD = 128
S_DEV = 8
CTX = 384
REQ = 1024


def draw_query(key, part):
    key = jax.random.fold_in(key, 1)
    values = jnp.clip(jax.random.normal(key, (REQ, HEADS * HD), jnp.float32), -6.0, 6.0)
    return values.astype(jnp.bfloat16)


def draw_key_cache(key, part):
    key = jax.random.fold_in(key, 2)
    values = jnp.clip(jax.random.normal(key, (REQ, CTX, KVH * HD), jnp.float32), -6.0, 6.0)
    return values.astype(jnp.bfloat16)


def draw_lengths(key, part):
    key = jax.random.fold_in(key, 3)
    base = jax.random.randint(jax.random.fold_in(key, 1), (REQ,), 0, CTX)
    factor = jax.random.randint(jax.random.fold_in(key, 2), (REQ // S_DEV,), 1, 5)
    factor_rows = jnp.repeat(factor, S_DEV)
    length = 1 + base * factor_rows // 4
    return jnp.where(jnp.arange(REQ) == 0, CTX, length).astype(jnp.int32)


def shard_levels(own_key, shape, cuts, least, top_value):
    def one(axis_at, shards_of):
        heights = jax.random.uniform(jax.random.fold_in(jax.random.fold_in(own_key, 6), axis_at), (shards_of,), jnp.float32, least / len(cuts), top_value / len(cuts))
        return jnp.repeat(jnp.exp(heights), shape[axis_at] // shards_of).reshape((-1,) + (1,) * (len(shape) - axis_at - 1))

    factor_of = one(*cuts[0])
    for cut in cuts[1:]:
        factor_of = factor_of * one(*cut)
    return factor_of


def gaussian(stream_key, dims, width, reach, cuts=(), kind=jnp.bfloat16):
    loudness = shard_levels(stream_key, dims, cuts, -0.22, 0.18) if cuts else 1.0
    values = jax.random.normal(stream_key, dims, jnp.float32) * width * loudness
    return jnp.minimum(jnp.maximum(values, -reach), reach).astype(kind)


def setup_inputs(seed: int = 0) -> dict:
    key_of = jax.random.split(jax.random.key(seed), 12)
    query = draw_query(jax.random.fold_in(key_of[11], 71), 0)
    new_key = gaussian(key_of[1], (REQ, KVH * HD), 1.0, 6.0, ((0, 128),))
    new_value = gaussian(key_of[2], (REQ, KVH * HD), 1.0, 6.0, ((0, 128),))
    key_cache = draw_key_cache(jax.random.fold_in(key_of[11], 71), 0)
    value_cache = gaussian(key_of[4], (REQ, CTX, KVH * HD), 1.0, 6.0, ((0, 128),))
    lengths = draw_lengths(jax.random.fold_in(key_of[11], 71), 0)
    residual = gaussian(key_of[6], (REQ, D), 1.0, 6.0, ((0, 128),), jnp.float32)
    norm_gain = jnp.clip(1.0 + 0.15 * jax.random.normal(key_of[7], (D,), jnp.float32), 0.25, 1.75)
    gate_weight = gaussian(key_of[8], (D, FF), D ** -0.5, 0.0625, ((0, 2), (1, 64)))
    up_weight = gaussian(key_of[9], (D, FF), D ** -0.5, 0.0625, ((0, 2), (1, 64)))
    down_weight = gaussian(key_of[10], (FF, D), FF ** -0.5, 0.03125, ((0, 64), (1, 2)))
    return dict(query=query, new_key=new_key, new_value=new_value, key_cache=key_cache, value_cache=value_cache, lengths=lengths, residual=residual, norm_gain=norm_gain, gate_weight=gate_weight, up_weight=up_weight, down_weight=down_weight)


def attend_one(items):
    query_row, key_rows, value_rows, key_new, value_new, length = items
    groups = HEADS // KVH
    scale = 1.0 / HD ** 0.5
    query_f = query_row.astype(jnp.float32).reshape(KVH, groups, HD)
    keys_f = key_rows.astype(jnp.float32).reshape(CTX, KVH, HD)
    values_f = value_rows.astype(jnp.float32).reshape(CTX, KVH, HD)
    key_new_f = key_new.astype(jnp.float32).reshape(KVH, HD)
    value_new_f = value_new.astype(jnp.float32).reshape(KVH, HD)
    scores = jnp.einsum('kgd,ckd->kgc', query_f, keys_f) * scale
    valid = jnp.arange(CTX, dtype=jnp.int32) < length
    scores = jnp.where(valid[None, None, :], scores, -jnp.inf)
    score_new = jnp.einsum('kgd,kd->kg', query_f, key_new_f) * scale
    peak = jnp.maximum(lax.optimization_barrier(jnp.max(scores, axis=-1)), score_new)
    probs = jnp.exp(scores - peak[..., None])
    prob_new = jnp.exp(score_new - peak)
    total = lax.optimization_barrier(jnp.sum(probs, axis=-1)) + prob_new
    probs_low = probs.astype(jnp.bfloat16).astype(jnp.float32)
    new_low = prob_new.astype(jnp.bfloat16).astype(jnp.float32)
    summed = jnp.einsum('kgc,ckd->kgd', probs_low, values_f) + new_low[..., None] * value_new_f[:, None, :]
    return (summed / total[..., None]).reshape(HEADS * HD)

def reference(query, new_key, new_value, key_cache, value_cache, lengths, residual, norm_gain, gate_weight, up_weight, down_weight):
    attn = lax.map(attend_one, (query, key_cache, value_cache, new_key, new_value, lengths))
    h_mid = residual + attn
    mean_sq = lax.optimization_barrier(jnp.mean(h_mid * h_mid, axis=-1, keepdims=True))
    normed = (h_mid * lax.rsqrt(mean_sq + 1e-05) * norm_gain[None, :]).astype(jnp.bfloat16)
    gate = jnp.dot(normed, gate_weight, preferred_element_type=jnp.float32)
    up = jnp.dot(normed, up_weight, preferred_element_type=jnp.float32)
    hidden = (jax.nn.silu(gate) * up).astype(jnp.bfloat16)
    ffn = jnp.dot(hidden, down_weight, preferred_element_type=jnp.float32)
    return (h_mid + ffn).astype(jnp.bfloat16)
```

```python
import jax
import jax.numpy as jnp
from jax import lax
from jax.experimental import pallas as pl
from jax.experimental.pallas import tpu as pltpu
from jax.sharding import PartitionSpec as P

HD = 128
SWAP = [(0, 1), (1, 0)]


def attend_kernel(
    lengths_ref, query_ref, new_key_ref, new_value_ref, key_ref, value_ref, residual_ref, gain_ref,
    mid_ref, normed_ref,
):
    per_step, heads, _ = query_ref.shape
    kv_heads = new_key_ref.shape[1]
    groups = heads // kv_heads
    ctx = key_ref.shape[1]
    scale = 1.0 / HD**0.5
    step = pl.program_id(0)
    row_group = lax.broadcasted_iota(jnp.int32, (heads, kv_heads * HD), 0) // groups
    col_group = lax.broadcasted_iota(jnp.int32, (heads, kv_heads * HD), 1) // HD
    own = row_group == col_group
    places = lax.broadcasted_iota(jnp.int32, (heads, ctx), 1)
    for slot in range(per_step):
        length = lengths_ref[step * per_step + slot]
        query = query_ref[slot]
        wide = jnp.where(own, jnp.concatenate([query] * kv_heads, axis=1), 0).astype(jnp.bfloat16)
        scores = (
            lax.dot_general(
                wide, key_ref[slot], (((1,), (1,)), ((), ())), preferred_element_type=jnp.float32
            )
            * scale
        )
        scores = jnp.where(places < length, scores, -jnp.inf)
        key_now = jnp.broadcast_to(
            new_key_ref[slot].astype(jnp.float32)[:, None, :], (kv_heads, groups, HD)
        ).reshape(heads, HD)
        value_now = jnp.broadcast_to(
            new_value_ref[slot].astype(jnp.float32)[:, None, :], (kv_heads, groups, HD)
        ).reshape(heads, HD)
        score_new = jnp.sum(query.astype(jnp.float32) * key_now, axis=1, keepdims=True) * scale
        peak = jnp.maximum(jnp.max(scores, axis=1, keepdims=True), score_new)
        probs = jnp.exp(scores - peak)
        prob_new = jnp.exp(score_new - peak)
        total = jnp.sum(probs, axis=1, keepdims=True) + prob_new
        spread = jnp.dot(
            probs.astype(jnp.bfloat16), value_ref[slot], preferred_element_type=jnp.float32
        )
        picked = jnp.concatenate(
            [
                spread[g * groups : (g + 1) * groups, g * HD : (g + 1) * HD]
                for g in range(kv_heads)
            ],
            axis=0,
        )
        summed = picked + prob_new.astype(jnp.bfloat16).astype(jnp.float32) * value_now
        mid = residual_ref[slot] + summed / total
        mid_ref[slot] = mid
        mean_sq = jnp.sum(jnp.sum(mid * mid, axis=1, keepdims=True), axis=0, keepdims=True) / (
            heads * HD
        )
        normed_ref[slot] = (mid * lax.rsqrt(mean_sq + 1e-05) * gain_ref[...]).astype(jnp.bfloat16)


def attend(query, new_key, new_value, key_cache, value_cache, lengths, residual, norm_gain):
    slots, width = query.shape
    heads = width // HD
    ctx, kv_width = key_cache.shape[1:]
    kv_heads = kv_width // HD
    per_step = 2 if slots % 2 == 0 else 1

    def rows(*shape):
        return pl.BlockSpec((per_step,) + shape, lambda i: (i,) + (0,) * len(shape))

    return pl.pallas_call(
        attend_kernel,
        grid=(slots // per_step,),
        in_specs=[
            pl.BlockSpec(memory_space=pltpu.SMEM),
            rows(heads, HD),
            rows(kv_heads, HD),
            rows(kv_heads, HD),
            rows(ctx, kv_width),
            rows(ctx, kv_width),
            rows(heads, HD),
            pl.BlockSpec((heads, HD), lambda i: (0, 0)),
        ],
        out_specs=[rows(heads, HD), rows(heads, HD)],
        out_shape=[
            jax.ShapeDtypeStruct((slots, heads, HD), jnp.float32),
            jax.ShapeDtypeStruct((slots, heads, HD), jnp.bfloat16),
        ],
        compiler_params=pltpu.CompilerParams(vmem_limit_bytes=40 * 1024 * 1024),
        name="attend",
    )(
        lengths,
        query.reshape(slots, heads, HD),
        new_key.reshape(slots, kv_heads, HD),
        new_value.reshape(slots, kv_heads, HD),
        key_cache,
        value_cache,
        residual.reshape(slots, heads, HD),
        norm_gain.reshape(heads, HD),
    )


def body(
    query,
    new_key,
    new_value,
    key_cache,
    value_cache,
    lengths,
    residual,
    norm_gain,
    gate_weight,
    up_weight,
    down_weight,
):
    slots, width = residual.shape
    half = gate_weight.shape[0]
    mid, normed = attend(
        query, new_key, new_value, key_cache, value_cache, lengths, residual, norm_gain
    )
    pair = lax.all_to_all(
        normed.reshape(slots, 2, half), "side", split_axis=1, concat_axis=0, tiled=True
    ).reshape(2 * slots, half)
    rows_all = lax.all_gather(pair, "gx", axis=0, tiled=True)
    gate_part = jnp.dot(rows_all, gate_weight, preferred_element_type=jnp.float32)
    up_part = jnp.dot(rows_all, up_weight, preferred_element_type=jnp.float32)
    gate_part, up_part = gate_part.astype(jnp.bfloat16), up_part.astype(jnp.bfloat16)
    gate = gate_part.astype(jnp.float32) + lax.ppermute(gate_part, "side", SWAP).astype(jnp.float32)
    up = up_part.astype(jnp.float32) + lax.ppermute(up_part, "side", SWAP).astype(jnp.float32)
    hidden = (jax.nn.silu(gate) * up).astype(jnp.bfloat16)
    partial = jnp.dot(hidden, down_weight, preferred_element_type=jnp.float32).astype(jnp.bfloat16)
    blocks = lax.all_to_all(
        partial.reshape(-1, 2 * slots, half), "gx", split_axis=0, concat_axis=0, tiled=True
    )
    summed = jnp.sum(blocks.astype(jnp.float32), axis=0).astype(jnp.bfloat16)
    ffn = lax.all_to_all(
        summed.reshape(2, slots, half), "side", split_axis=0, concat_axis=2, tiled=True
    ).reshape(slots, width)
    return (mid.reshape(slots, width) + ffn.astype(jnp.float32)).astype(jnp.bfloat16)


def solution(mesh):
    in_specs = (
        P(("side", "gx"), None),
        P(("side", "gx"), None),
        P(("side", "gx"), None),
        P(("side", "gx"), None, None),
        P(("side", "gx"), None, None),
        P(("side", "gx")),
        P(("side", "gx"), None),
        P(),
        P("side", "gx"),
        P("side", "gx"),
        P("gx", "side"),
    )
    out_specs = P(("side", "gx"), None)
    return jax.shard_map(body, mesh=mesh, in_specs=in_specs, out_specs=out_specs, check_vma=False)
```

```python
import functools

import jax
import jax.numpy as jnp
from jax import lax
from jax.experimental import pallas as pl
from jax.experimental.pallas import tpu as pltpu
from jax.sharding import PartitionSpec as P

HD = 128
SWAP = [(0, 1), (1, 0)]
RING = 4
VMEM = 60 * 1024 * 1024
NEAR, FAR = (0, 1, 3), 2
LINES = {"first": ("x", "z"), "second": ("z", "y"), "third": ("y", "x")}


def chip(z, x, y):
    return (z % RING) * RING * RING + (x % RING) * RING + y % RING


def hops(line, distance):
    pairs = []
    for side in range(2):
        dz, dx, dy = (distance * (axis == LINES[line][side]) for axis in "zxy")
        for z in range(RING):
            for x in range(RING):
                for y in range(RING):
                    here, there = chip(z, x, y), chip(z + dz, x + dx, y + dy)
                    pairs.append((side * RING**3 + here, side * RING**3 + there))
    return pairs


def send(array, line, distance):
    return lax.ppermute(array, ("side", "gx"), hops(line, distance))


def fetch(array, line, distance):
    return lax.ppermute(array, ("side", "gx"), [(there, here) for here, there in hops(line, distance)])


def gather_line(array, line):
    far = fetch(array, line, 2)
    return [array, fetch(array, line, 1), far, fetch(array, line, 3)]


def gather_ring(top, bottom, line):
    after_top, before_bottom = fetch(top, line, 1), fetch(bottom, line, 3)
    after_bottom, before_top = fetch(bottom, line, 1), fetch(top, line, 3)
    far = [fetch(after_top, line, 1), fetch(before_bottom, line, 3)]
    return [[top, bottom], [after_top, after_bottom], far, [before_top, before_bottom]]


def behind(array, *others):
    return lax.optimization_barrier((array, *others))[0]


def add(*arrays):
    return sum(array.astype(jnp.float32) for array in arrays).astype(jnp.bfloat16)


def reduce_line(blocks, line):
    far = send(blocks[2], line, 2)
    return add(blocks[0], send(blocks[1], line, 1), far, send(blocks[3], line, 3))


def parts(array):
    rows = array.shape[0] // RING
    return [array[i * rows : (i + 1) * rows] for i in range(RING)]


def dot(left, right):
    return jnp.dot(left, right, preferred_element_type=jnp.float32)


def attend_kernel(
    lengths_ref, query_ref, new_key_ref, new_value_ref, key_ref, value_ref, residual_ref, gain_ref,
    mid_ref, normed_ref,
):
    per_step, heads, _ = query_ref.shape
    kv_heads = new_key_ref.shape[1]
    groups = heads // kv_heads
    ctx = key_ref.shape[1]
    scale = 1.0 / HD**0.5
    step = pl.program_id(0)
    row_group = lax.broadcasted_iota(jnp.int32, (heads, kv_heads * HD), 0) // groups
    col_group = lax.broadcasted_iota(jnp.int32, (heads, kv_heads * HD), 1) // HD
    own = row_group == col_group
    places = lax.broadcasted_iota(jnp.int32, (heads, ctx), 1)
    for slot in range(per_step):
        length = lengths_ref[step * per_step + slot]
        query = query_ref[slot]
        wide = jnp.where(own, jnp.concatenate([query] * kv_heads, axis=1), 0).astype(jnp.bfloat16)
        scores = (
            lax.dot_general(
                wide, key_ref[slot], (((1,), (1,)), ((), ())), preferred_element_type=jnp.float32
            )
            * scale
        )
        scores = jnp.where(places < length, scores, -jnp.inf)
        key_now = jnp.broadcast_to(
            new_key_ref[slot].astype(jnp.float32)[:, None, :], (kv_heads, groups, HD)
        ).reshape(heads, HD)
        value_now = jnp.broadcast_to(
            new_value_ref[slot].astype(jnp.float32)[:, None, :], (kv_heads, groups, HD)
        ).reshape(heads, HD)
        score_new = jnp.sum(query.astype(jnp.float32) * key_now, axis=1, keepdims=True) * scale
        peak = jnp.maximum(jnp.max(scores, axis=1, keepdims=True), score_new)
        probs = jnp.exp(scores - peak)
        prob_new = jnp.exp(score_new - peak)
        total = jnp.sum(probs, axis=1, keepdims=True) + prob_new
        spread = jnp.dot(
            probs.astype(jnp.bfloat16), value_ref[slot], preferred_element_type=jnp.float32
        )
        picked = jnp.concatenate(
            [
                spread[g * groups : (g + 1) * groups, g * HD : (g + 1) * HD]
                for g in range(kv_heads)
            ],
            axis=0,
        )
        summed = picked + prob_new.astype(jnp.bfloat16).astype(jnp.float32) * value_now
        mid = residual_ref[slot] + summed / total
        mid_ref[slot] = mid
        mean_sq = jnp.sum(jnp.sum(mid * mid, axis=1, keepdims=True), axis=0, keepdims=True) / (
            heads * HD
        )
        normed_ref[slot] = (mid * lax.rsqrt(mean_sq + 1e-05) * gain_ref[...]).astype(jnp.bfloat16)


def attend(query, new_key, new_value, key_cache, value_cache, lengths, residual, norm_gain):
    slots, width = query.shape
    heads = width // HD
    ctx, kv_width = key_cache.shape[1:]
    kv_heads = kv_width // HD
    per_step = 2 if slots % 2 == 0 else 1

    def rows(*shape):
        return pl.BlockSpec((per_step,) + shape, lambda i: (i,) + (0,) * len(shape))

    return pl.pallas_call(
        attend_kernel,
        grid=(slots // per_step,),
        in_specs=[
            pl.BlockSpec(memory_space=pltpu.SMEM),
            rows(heads, HD),
            rows(kv_heads, HD),
            rows(kv_heads, HD),
            rows(ctx, kv_width),
            rows(ctx, kv_width),
            rows(heads, HD),
            pl.BlockSpec((heads, HD), lambda i: (0, 0)),
        ],
        out_specs=[rows(heads, HD), rows(heads, HD)],
        out_shape=[
            jax.ShapeDtypeStruct((slots, heads, HD), jnp.float32),
            jax.ShapeDtypeStruct((slots, heads, HD), jnp.bfloat16),
        ],
        compiler_params=pltpu.CompilerParams(vmem_limit_bytes=VMEM),
        name="attend",
    )(
        lengths,
        query.reshape(slots, heads, HD),
        new_key.reshape(slots, kv_heads, HD),
        new_value.reshape(slots, kv_heads, HD),
        key_cache,
        value_cache,
        residual.reshape(slots, heads, HD),
        norm_gain.reshape(heads, HD),
    )


def times(rows, weight):
    return lax.dot_general(rows, weight, (((1,), (1,)), ((), ())), preferred_element_type=jnp.float32)


def project_kernel(*refs):
    *half_refs, gate_ref, up_ref, out_ref, gate_total, up_total = refs
    step = pl.program_id(0)
    units = gate_ref.shape[0]
    rows = jnp.concatenate([ref[...] for ref in half_refs], axis=0)
    gate, up = times(rows, gate_ref[...]), times(rows, up_ref[...])

    @pl.when(step == 0)
    def _():
        gate_total[...] = gate
        up_total[...] = up

    @pl.when(step > 0)
    def _():
        gate_total[...] += gate
        up_total[...] += up

    @pl.when(step == pl.num_programs(0) - 1)
    def _():
        shape = out_ref.shape[:2] + (units,)
        out_ref[:, :, :units] = gate_total[...].astype(jnp.bfloat16).reshape(shape)
        out_ref[:, :, units:] = up_total[...].astype(jnp.bfloat16).reshape(shape)


def project(blocks, gate_weight, up_weight, chunk):
    cut, features = blocks[0][0].shape
    units = gate_weight.shape[0]
    count = len(blocks)
    weights = pl.BlockSpec((units, chunk), lambda i: (0, i))
    return pl.pallas_call(
        project_kernel,
        grid=(features // chunk,),
        in_specs=[pl.BlockSpec((cut, chunk), lambda i: (0, i)) for _ in range(2 * count)]
        + [weights, weights],
        out_specs=pl.BlockSpec((count, 2 * cut, 2 * units), lambda i: (0, 0, 0)),
        out_shape=jax.ShapeDtypeStruct((count, 2 * cut, 2 * units), jnp.bfloat16),
        scratch_shapes=[pltpu.VMEM((count * 2 * cut, units), jnp.float32)] * 2,
        compiler_params=pltpu.CompilerParams(vmem_limit_bytes=24 * 1024 * 1024),
        cost_estimate=pl.CostEstimate(
            flops=8 * count * cut * units * features,
            bytes_accessed=4 * units * features,
            transcendentals=0,
        ),
        name="project",
    )(*[half for block in blocks for half in block], gate_weight, up_weight)


def combine_kernel(side_ref, own_near, own_far, got_near, got_far, hidden_ref):
    units = hidden_ref.shape[-1]
    even = side_ref[0] == 0

    def pick(near, far, third, second, first):
        if third == FAR:
            return far[0, second, first].astype(jnp.float32)
        return near[NEAR.index(third), second, first].astype(jnp.float32)

    for third in range(RING):
        for second in range(RING):
            for first in range(RING):
                got = jnp.where(
                    even,
                    pick(got_near, got_far, first, third, second),
                    pick(got_near, got_far, second, first, third),
                )
                both = pick(own_near, own_far, third, second, first) + got
                gate, up = both[:, :units], both[:, units:]
                hidden = gate / (1.0 + jnp.exp(-gate)) * up
                hidden_ref[third, second, first] = hidden.astype(jnp.bfloat16)


def combine(side, *halves):
    rows, both = halves[0].shape[-2:]
    return pl.pallas_call(
        combine_kernel,
        in_specs=[pl.BlockSpec(memory_space=pltpu.SMEM)]
        + [pl.BlockSpec(memory_space=pltpu.VMEM) for _ in halves],
        out_specs=pl.BlockSpec(memory_space=pltpu.VMEM),
        out_shape=jax.ShapeDtypeStruct((RING, RING, RING, rows, both // 2), jnp.bfloat16),
        compiler_params=pltpu.CompilerParams(vmem_limit_bytes=24 * 1024 * 1024),
        name="combine",
    )(side, *halves)


def body(
    query,
    new_key,
    new_value,
    key_cache,
    value_cache,
    lengths,
    residual,
    norm_gain,
    gate_weight,
    up_weight,
    down_weight,
):
    slots, width = residual.shape
    half = gate_weight.shape[0]
    hidden_units = gate_weight.shape[1]
    rows = 2 * slots
    side = lax.axis_index("side")
    mid, normed = attend(
        query, new_key, new_value, key_cache, value_cache, lengths, residual, norm_gain
    )
    pair = lax.all_to_all(
        normed.reshape(slots, 2, half), "side", split_axis=1, concat_axis=0, tiled=True
    ).reshape(rows, half)

    near = jnp.concatenate(gather_line(pair, "first"), axis=0)
    planes = gather_line(near, "second")
    top, bottom = jnp.concatenate(planes[:2], axis=0), jnp.concatenate(planes[2:], axis=0)
    blocks = gather_ring(top, bottom, "third")

    near = project([blocks[third] for third in NEAR], gate_weight.T, up_weight.T, half // 8)
    far = [behind(run, near) for run in blocks[FAR]]
    far = project([far], gate_weight.T, up_weight.T, half // 4)
    halves = [near, far, lax.ppermute(near, "side", SWAP), lax.ppermute(far, "side", SWAP)]
    hidden = combine(
        side.reshape(1), *[h.reshape(-1, RING, RING, rows, 2 * hidden_units) for h in halves]
    )

    cut = RING * RING * rows // 2
    runs = [hidden[third].reshape(2, cut, hidden_units) for third in range(RING)]

    def down(run):
        return dot(run.reshape(-1, hidden_units), down_weight).astype(jnp.bfloat16)

    part_far = down(runs[FAR])
    after, before = send(part_far[:cut], "third", 1), send(part_far[cut:], "third", 3)
    one_bottom = send(down(behind(runs[1][1], part_far)), "third", 1)
    three_top = send(down(behind(runs[3][0], part_far)), "third", 3)
    one_top = down(behind(runs[1][0], part_far))
    three_bottom = down(behind(runs[3][1], part_far))
    part_own = down(behind(runs[0], part_far))
    one_top = send(add(one_top, after), "third", 1)
    three_bottom = send(add(three_bottom, before), "third", 3)
    summed = [
        add(part_own[:cut], one_top, three_top),
        add(part_own[cut:], one_bottom, three_bottom),
    ]
    summed = [run for part in summed for run in (part[: cut // 2], part[cut // 2 :])]
    summed = reduce_line(summed, "second")
    summed = reduce_line(parts(summed), "first")

    by_side = summed.reshape(2, slots, half)
    kept = lax.dynamic_index_in_dim(by_side, side, 0, keepdims=False)
    got = lax.ppermute(lax.dynamic_index_in_dim(by_side, 1 - side, 0, keepdims=False), "side", SWAP)
    ffn = jnp.concatenate([jnp.where(side == 0, kept, got), jnp.where(side == 0, got, kept)], axis=1)
    return (mid.reshape(slots, width) + ffn.astype(jnp.float32)).astype(jnp.bfloat16)


def solution(mesh):
    in_specs = (
        P(("side", "gx"), None),
        P(("side", "gx"), None),
        P(("side", "gx"), None),
        P(("side", "gx"), None, None),
        P(("side", "gx"), None, None),
        P(("side", "gx")),
        P(("side", "gx"), None),
        P(),
        P("side", "gx"),
        P("side", "gx"),
        P("gx", "side"),
    )
    out_specs = P(("side", "gx"), None)
    return jax.shard_map(body, mesh=mesh, in_specs=in_specs, out_specs=out_specs, check_vma=False)
```

```python
import functools

import jax
import jax.numpy as jnp
from jax import lax
from jax.experimental import pallas as pl
from jax.experimental.pallas import tpu as pltpu
from jax.sharding import PartitionSpec as P

HD = 128
SWAP = [(0, 1), (1, 0)]
RING = 4
VMEM = 60 * 1024 * 1024
TOGETHER = 4
FAR = 2
PLACE = {(0, 0): (0, 0), (0, 1): (0, 1), (1, 0): (1, 0), (3, 1): (1, 1), (1, 1): (2, 0), (3, 0): (2, 1)}
LINES = {"first": ("x", "z"), "second": ("z", "y"), "third": ("y", "x")}


def chip(z, x, y):
    return (z % RING) * RING * RING + (x % RING) * RING + y % RING


def hops(line, distance):
    pairs = []
    for side in range(2):
        dz, dx, dy = (distance * (axis == LINES[line][side]) for axis in "zxy")
        for z in range(RING):
            for x in range(RING):
                for y in range(RING):
                    here, there = chip(z, x, y), chip(z + dz, x + dx, y + dy)
                    pairs.append((side * RING**3 + here, side * RING**3 + there))
    return pairs


def send(array, line, distance):
    return lax.ppermute(array, ("side", "gx"), hops(line, distance))


def fetch(array, line, distance):
    return lax.ppermute(array, ("side", "gx"), [(there, here) for here, there in hops(line, distance)])


def gather_line(array, line):
    far = fetch(array, line, 2)
    return [array, fetch(array, line, 1), far, fetch(array, line, 3)]


def gather_ring(top, bottom, line):
    after_top, before_bottom = fetch(top, line, 1), fetch(bottom, line, 3)
    after_bottom, before_top = fetch(bottom, line, 1), fetch(top, line, 3)
    far = [fetch(after_top, line, 1), fetch(before_bottom, line, 3)]
    return [[top, bottom], [after_top, after_bottom], far, [before_top, before_bottom]]


def behind(array, *others):
    return lax.optimization_barrier((array, *others))[0]


def add(*arrays):
    return sum(array.astype(jnp.float32) for array in arrays).astype(jnp.bfloat16)


def reduce_line(blocks, line):
    far = send(blocks[2], line, 2)
    return add(blocks[0], send(blocks[1], line, 1), far, send(blocks[3], line, 3))


def parts(array):
    rows = array.shape[0] // RING
    return [array[i * rows : (i + 1) * rows] for i in range(RING)]


def dot(left, right):
    return jnp.dot(left, right, preferred_element_type=jnp.float32)


def attend_kernel(
    side_ref, lengths_ref, query_ref, new_key_ref, new_value_ref, residual_ref, gain_ref,
    key_cache, value_cache, mid_ref, own_ref, other_ref,
    key_ref, value_ref, copied, queries, keys_now, values_now,
):
    heads, slots, _ = query_ref.shape
    kv_heads = new_key_ref.shape[0]
    groups = heads // kv_heads
    ctx = key_ref.shape[1]
    scale = 1.0 / HD**0.5
    runs = [range(start, min(start + TOGETHER, slots)) for start in range(0, slots, TOGETHER)]

    def copy(kind, slot):
        cache, held = ((key_cache, key_ref), (value_cache, value_ref))[kind]
        return pltpu.make_async_copy(cache.at[slot], held.at[slot], copied.at[kind, slot])

    for run in runs:
        for kind in range(2):
            for slot in run:
                copy(kind, slot).start()
    queries[...] = query_ref[...].astype(jnp.float32)
    keys_now[...] = new_key_ref[...].astype(jnp.float32)
    values_now[...] = new_value_ref[...].astype(jnp.float32)

    def spread_heads(rows):
        return jnp.broadcast_to(rows[:, None, :], (kv_heads, groups, HD)).reshape(heads, HD)

    row_group = lax.broadcasted_iota(jnp.int32, (heads, kv_heads * HD), 0) // groups
    col_group = lax.broadcasted_iota(jnp.int32, (heads, kv_heads * HD), 1) // HD
    own = row_group == col_group
    places = lax.broadcasted_iota(jnp.int32, (heads, ctx), 1)
    for run in runs:
        query_of, scores_of, probs_of, new_of, total_of = {}, {}, {}, {}, {}
        for slot in run:
            copy(0, slot).wait()
        for slot in run:
            query_of[slot] = queries[:, slot, :]
            wide = jnp.where(own, jnp.concatenate([query_of[slot]] * kv_heads, axis=1), 0)
            scores_of[slot] = lax.dot_general(
                wide.astype(jnp.bfloat16),
                key_ref[slot],
                (((1,), (1,)), ((), ())),
                preferred_element_type=jnp.float32,
            )
        for slot in run:
            scores = jnp.where(places < lengths_ref[slot], scores_of[slot] * scale, -jnp.inf)
            key_now = spread_heads(keys_now[:, slot, :])
            score_new = jnp.sum(query_of[slot] * key_now, axis=1, keepdims=True) * scale
            peak = jnp.maximum(jnp.max(scores, axis=1, keepdims=True), score_new)
            probs = jnp.exp(scores - peak)
            prob_new = jnp.exp(score_new - peak)
            total_of[slot] = jnp.sum(probs, axis=1, keepdims=True) + prob_new
            probs_of[slot] = probs.astype(jnp.bfloat16)
            new_of[slot] = prob_new.astype(jnp.bfloat16).astype(jnp.float32)
        for slot in run:
            copy(1, slot).wait()
        for slot in run:
            value_now = spread_heads(values_now[:, slot, :])
            spread = jnp.dot(probs_of[slot], value_ref[slot], preferred_element_type=jnp.float32)
            picked = jnp.concatenate(
                [
                    spread[g * groups : (g + 1) * groups, g * HD : (g + 1) * HD]
                    for g in range(kv_heads)
                ],
                axis=0,
            )
            summed = picked + new_of[slot] * value_now
            mid_ref[:, slot, :] = summed / total_of[slot]

    mid = residual_ref[...] + mid_ref[...]
    mid_ref[...] = mid
    squares = jnp.sum(jnp.sum(mid * mid, axis=0, keepdims=True), axis=2, keepdims=True)
    mean_sq = squares / (heads * HD)
    normed = (mid * lax.rsqrt(mean_sq + 1e-05) * gain_ref[...]).astype(jnp.bfloat16)
    halves = normed[: heads // 2], normed[heads // 2 :]
    even = side_ref[0] == 0
    own_ref[...] = jnp.where(even, halves[0], halves[1])
    other_ref[...] = jnp.where(even, halves[1], halves[0])


def attend(side, query, new_key, new_value, key_cache, value_cache, lengths, residual, norm_gain):
    slots, width = query.shape
    heads = width // HD

    def by_head(array):
        return array.reshape(slots, -1, HD).transpose(1, 0, 2)

    smem, vmem = (pl.BlockSpec(memory_space=space) for space in (pltpu.SMEM, pltpu.VMEM))
    kv_shape = (new_key.shape[1] // HD, slots, HD)
    half = jax.ShapeDtypeStruct((heads // 2, slots, HD), jnp.bfloat16)
    return pl.pallas_call(
        attend_kernel,
        in_specs=[smem, smem] + [vmem] * 5 + [pl.BlockSpec(memory_space=pl.ANY)] * 2,
        out_specs=[vmem] * 3,
        out_shape=[jax.ShapeDtypeStruct((heads, slots, HD), jnp.float32), half, half],
        scratch_shapes=[
            pltpu.VMEM(key_cache.shape, jnp.bfloat16),
            pltpu.VMEM(value_cache.shape, jnp.bfloat16),
            pltpu.SemaphoreType.DMA((2, slots)),
            pltpu.VMEM((heads, slots, HD), jnp.float32),
            pltpu.VMEM(kv_shape, jnp.float32),
            pltpu.VMEM(kv_shape, jnp.float32),
        ],
        compiler_params=pltpu.CompilerParams(vmem_limit_bytes=VMEM),
        name="attend",
    )(
        side.reshape(1),
        lengths,
        by_head(query),
        by_head(new_key),
        by_head(new_value),
        by_head(residual),
        norm_gain.reshape(heads, 1, HD),
        key_cache,
        value_cache,
    )


def times(rows, weight):
    return lax.dot_general(rows, weight, (((1,), (1,)), ((), ())), preferred_element_type=jnp.float32)


def project_kernel(*refs):
    top_ref, bottom_ref, gate_ref, up_ref, out_ref = refs[-5:]
    units = gate_ref.shape[0]
    shape = out_ref.shape[1:3] + (units,)
    rows = jnp.concatenate([top_ref[...], bottom_ref[...]], axis=0)
    out_ref[0, :, :, :units] = times(rows, gate_ref[...]).astype(jnp.bfloat16).reshape(shape)
    out_ref[0, :, :, units:] = times(rows, up_ref[...]).astype(jnp.bfloat16).reshape(shape)


def project(found, place, count, halves, gate_weight, up_weight):
    cut, features = halves[0].shape
    units = gate_weight.shape[0]
    vmem = pl.BlockSpec(memory_space=pltpu.VMEM)
    earlier = [] if found is None else [found]
    return pl.pallas_call(
        project_kernel,
        grid=(1,),
        in_specs=[pl.BlockSpec(memory_space=pl.ANY) for _ in earlier] + [vmem] * 4,
        out_specs=pl.BlockSpec((1, 2, cut, 2 * units), lambda i: (place, 0, 0, 0)),
        out_shape=jax.ShapeDtypeStruct((count, 2, cut, 2 * units), jnp.bfloat16),
        input_output_aliases={0: 0} if earlier else {},
        compiler_params=pltpu.CompilerParams(vmem_limit_bytes=24 * 1024 * 1024),
        cost_estimate=pl.CostEstimate(
            flops=8 * cut * units * features, bytes_accessed=4 * units * features, transcendentals=0
        ),
        name="project",
    )(*earlier, *halves, gate_weight, up_weight)


def combine_kernel(side_ref, own_near, own_far, got_near, got_far, hidden_ref):
    units = hidden_ref.shape[-1]
    even = side_ref[0] == 0

    def pick(near, far, third, second, first):
        half, inner = divmod(second, RING // 2)
        if third == FAR:
            return far[0, half, inner, first].astype(jnp.float32)
        place, at = PLACE[third, half]
        return near[place, at, inner, first].astype(jnp.float32)

    for third in range(RING):
        for second in range(RING):
            for first in range(RING):
                got = jnp.where(
                    even,
                    pick(got_near, got_far, first, third, second),
                    pick(got_near, got_far, second, first, third),
                )
                both = pick(own_near, own_far, third, second, first) + got
                gate, up = both[:, :units], both[:, units:]
                hidden = gate / (1.0 + jnp.exp(-gate)) * up
                hidden_ref[third, second, first] = hidden.astype(jnp.bfloat16)


def combine(side, *halves):
    rows, both = halves[0].shape[-2:]
    return pl.pallas_call(
        combine_kernel,
        in_specs=[pl.BlockSpec(memory_space=pltpu.SMEM)]
        + [pl.BlockSpec(memory_space=pltpu.VMEM) for _ in halves],
        out_specs=pl.BlockSpec(memory_space=pltpu.VMEM),
        out_shape=jax.ShapeDtypeStruct((RING, RING, RING, rows, both // 2), jnp.bfloat16),
        compiler_params=pltpu.CompilerParams(vmem_limit_bytes=24 * 1024 * 1024),
        name="combine",
    )(side, *halves)


def body(
    query,
    new_key,
    new_value,
    key_cache,
    value_cache,
    lengths,
    residual,
    norm_gain,
    gate_weight,
    up_weight,
    down_weight,
):
    slots, width = residual.shape
    half = gate_weight.shape[0]
    hidden_units = gate_weight.shape[1]
    rows = 2 * slots
    side = lax.axis_index("side")
    even = side == 0
    mid, own, other = attend(
        side, query, new_key, new_value, key_cache, value_cache, lengths, residual, norm_gain
    )
    got = lax.ppermute(other, "side", SWAP)
    pair = jnp.stack([jnp.where(even, own, got), jnp.where(even, got, own)])
    pair = pair.transpose(0, 2, 1, 3).reshape(rows, half)

    near = jnp.concatenate(gather_line(pair, "first"), axis=0)
    planes = gather_line(near, "second")
    top, bottom = jnp.concatenate(planes[:2], axis=0), jnp.concatenate(planes[2:], axis=0)
    blocks = gather_ring(top, bottom, "third")

    weights = gate_weight.T, up_weight.T
    near = None
    for place in range(3):
        pieces = [blocks[third][part] for (third, part), at in PLACE.items() if at[0] == place]
        near = project(near, place, 3, pieces, *weights)
    far = project(None, 0, 1, [behind(run, near) for run in blocks[FAR]], *weights)
    halves = [near, far, lax.ppermute(near, "side", SWAP), lax.ppermute(far, "side", SWAP)]
    hidden = combine(
        side.reshape(1), *[h.reshape(-1, 2, RING // 2, RING, rows, 2 * hidden_units) for h in halves]
    )

    cut = RING * RING * rows // 2
    runs = [hidden[third].reshape(2, cut, hidden_units) for third in range(RING)]

    def down(run):
        return dot(run.reshape(-1, hidden_units), down_weight).astype(jnp.bfloat16)

    part_far = down(runs[FAR])
    after, before = send(part_far[:cut], "third", 1), send(part_far[cut:], "third", 3)
    one_bottom = send(down(behind(runs[1][1], part_far)), "third", 1)
    three_top = send(down(behind(runs[3][0], part_far)), "third", 3)
    one_top = down(behind(runs[1][0], part_far))
    three_bottom = down(behind(runs[3][1], part_far))
    part_own = down(behind(runs[0], part_far))
    one_top = send(add(one_top, after), "third", 1)
    three_bottom = send(add(three_bottom, before), "third", 3)
    summed = [
        add(part_own[:cut], one_top, three_top),
        add(part_own[cut:], one_bottom, three_bottom),
    ]
    summed = [run for part in summed for run in (part[: cut // 2], part[cut // 2 :])]
    summed = reduce_line(summed, "second")
    summed = reduce_line(parts(summed), "first")

    by_side = summed.reshape(2, slots, half)
    kept = lax.dynamic_index_in_dim(by_side, side, 0, keepdims=False)
    got = lax.ppermute(lax.dynamic_index_in_dim(by_side, 1 - side, 0, keepdims=False), "side", SWAP)
    ffn = jnp.concatenate([jnp.where(even, kept, got), jnp.where(even, got, kept)], axis=1)
    mid = mid.transpose(1, 0, 2).reshape(slots, width)
    return (mid + ffn.astype(jnp.float32)).astype(jnp.bfloat16)


def solution(mesh):
    in_specs = (
        P(("side", "gx"), None),
        P(("side", "gx"), None),
        P(("side", "gx"), None),
        P(("side", "gx"), None, None),
        P(("side", "gx"), None, None),
        P(("side", "gx")),
        P(("side", "gx"), None),
        P(),
        P("side", "gx"),
        P("side", "gx"),
        P("gx", "side"),
    )
    out_specs = P(("side", "gx"), None)
    return jax.shard_map(body, mesh=mesh, in_specs=in_specs, out_specs=out_specs, check_vma=False)
```

```python
import functools

import jax
import jax.numpy as jnp
from jax import lax
from jax.experimental import pallas as pl
from jax.experimental.pallas import tpu as pltpu
from jax.sharding import PartitionSpec as P

HD = 128
SWAP = [(0, 1), (1, 0)]
RING = 4
VMEM = 60 * 1024 * 1024
TOGETHER = 4
FAR = 2
ORDER = (0, 1, 3, 2)
STEPS = (0, 1, 3, 2)
FAR = 2
PLACE = {(0, 0): (0, 0), (0, 1): (0, 1), (1, 0): (1, 0), (3, 1): (1, 1), (1, 1): (2, 0), (3, 0): (2, 1)}
LINES = {"first": ("x", "z"), "second": ("z", "y"), "third": ("y", "x")}


def chip(z, x, y):
    return (z % RING) * RING * RING + (x % RING) * RING + y % RING


def hops(line, distance):
    pairs = []
    for side in range(2):
        dz, dx, dy = (distance * (axis == LINES[line][side]) for axis in "zxy")
        for z in range(RING):
            for x in range(RING):
                for y in range(RING):
                    here, there = chip(z, x, y), chip(z + dz, x + dx, y + dy)
                    pairs.append((side * RING**3 + here, side * RING**3 + there))
    return pairs


def send(array, line, distance):
    return lax.ppermute(array, ("side", "gx"), hops(line, distance))


def fetch(array, line, distance):
    return lax.ppermute(array, ("side", "gx"), [(there, here) for here, there in hops(line, distance)])


def gather_line(array, line):
    far = fetch(array, line, 2)
    return [array, fetch(array, line, 1), far, fetch(array, line, 3)]


def gather_ring(early, late, line):
    step = late.shape[0]
    after, before = fetch(early, line, 1), fetch(early, line, 3)
    after_late, before_late = fetch(late, line, 1), fetch(late, line, 3)
    far = [
        fetch(after[: 2 * step], line, 1),
        fetch(before[2 * step :], line, 3),
        fetch(behind(before_late, after_late), line, 3),
    ]
    return [[early, late], [after, after_late], far, [before, before_late]]


def behind(array, *others):
    return lax.optimization_barrier((array, *others))[0]


def add(*arrays):
    return sum(array.astype(jnp.float32) for array in arrays).astype(jnp.bfloat16)


def reduce_line(blocks, line):
    far = send(blocks[2], line, 2)
    return add(blocks[0], send(blocks[1], line, 1), far, send(blocks[3], line, 3))


def parts(array):
    rows = array.shape[0] // RING
    return [array[i * rows : (i + 1) * rows] for i in range(RING)]


def dot(left, right):
    return jnp.dot(left, right, preferred_element_type=jnp.float32)


def attend_kernel(
    side_ref, lengths_ref, query_ref, new_key_ref, new_value_ref, residual_ref, gain_ref,
    key_cache, value_cache, mid_ref, own_ref, other_ref,
    key_ref, value_ref, copied, queries, keys_now, values_now,
):
    heads, slots, _ = query_ref.shape
    kv_heads = new_key_ref.shape[0]
    groups = heads // kv_heads
    ctx = key_ref.shape[1]
    scale = 1.0 / HD**0.5
    runs = [range(start, min(start + TOGETHER, slots)) for start in range(0, slots, TOGETHER)]

    def copy(kind, slot):
        cache, held = ((key_cache, key_ref), (value_cache, value_ref))[kind]
        return pltpu.make_async_copy(cache.at[slot], held.at[slot], copied.at[kind, slot])

    for run in runs:
        for kind in range(2):
            for slot in run:
                copy(kind, slot).start()
    queries[...] = query_ref[...].astype(jnp.float32)
    keys_now[...] = new_key_ref[...].astype(jnp.float32)
    values_now[...] = new_value_ref[...].astype(jnp.float32)

    def spread_heads(rows):
        return jnp.broadcast_to(rows[:, None, :], (kv_heads, groups, HD)).reshape(heads, HD)

    row_group = lax.broadcasted_iota(jnp.int32, (heads, kv_heads * HD), 0) // groups
    col_group = lax.broadcasted_iota(jnp.int32, (heads, kv_heads * HD), 1) // HD
    own = row_group == col_group
    places = lax.broadcasted_iota(jnp.int32, (heads, ctx), 1)
    for run in runs:
        query_of, scores_of, probs_of, new_of, total_of = {}, {}, {}, {}, {}
        for slot in run:
            copy(0, slot).wait()
        for slot in run:
            query_of[slot] = queries[:, slot, :]
            wide = jnp.where(own, jnp.concatenate([query_of[slot]] * kv_heads, axis=1), 0)
            scores_of[slot] = lax.dot_general(
                wide.astype(jnp.bfloat16),
                key_ref[slot],
                (((1,), (1,)), ((), ())),
                preferred_element_type=jnp.float32,
            )
        for slot in run:
            scores = jnp.where(places < lengths_ref[slot], scores_of[slot] * scale, -jnp.inf)
            key_now = spread_heads(keys_now[:, slot, :])
            score_new = jnp.sum(query_of[slot] * key_now, axis=1, keepdims=True) * scale
            peak = jnp.maximum(jnp.max(scores, axis=1, keepdims=True), score_new)
            probs = jnp.exp(scores - peak)
            prob_new = jnp.exp(score_new - peak)
            total_of[slot] = jnp.sum(probs, axis=1, keepdims=True) + prob_new
            probs_of[slot] = probs.astype(jnp.bfloat16)
            new_of[slot] = prob_new.astype(jnp.bfloat16).astype(jnp.float32)
        for slot in run:
            copy(1, slot).wait()
        for slot in run:
            value_now = spread_heads(values_now[:, slot, :])
            spread = jnp.dot(probs_of[slot], value_ref[slot], preferred_element_type=jnp.float32)
            picked = jnp.concatenate(
                [
                    spread[g * groups : (g + 1) * groups, g * HD : (g + 1) * HD]
                    for g in range(kv_heads)
                ],
                axis=0,
            )
            summed = picked + new_of[slot] * value_now
            mid_ref[:, slot, :] = summed / total_of[slot]

    mid = residual_ref[...] + mid_ref[...]
    mid_ref[...] = mid
    squares = jnp.sum(jnp.sum(mid * mid, axis=0, keepdims=True), axis=2, keepdims=True)
    mean_sq = squares / (heads * HD)
    normed = (mid * lax.rsqrt(mean_sq + 1e-05) * gain_ref[...]).astype(jnp.bfloat16)
    halves = normed[: heads // 2], normed[heads // 2 :]
    even = side_ref[0] == 0
    own_ref[...] = jnp.where(even, halves[0], halves[1])
    other_ref[...] = jnp.where(even, halves[1], halves[0])


def attend(side, query, new_key, new_value, key_cache, value_cache, lengths, residual, norm_gain):
    slots, width = query.shape
    heads = width // HD

    def by_head(array):
        return array.reshape(slots, -1, HD).transpose(1, 0, 2)

    smem, vmem = (pl.BlockSpec(memory_space=space) for space in (pltpu.SMEM, pltpu.VMEM))
    kv_shape = (new_key.shape[1] // HD, slots, HD)
    half = jax.ShapeDtypeStruct((heads // 2, slots, HD), jnp.bfloat16)
    return pl.pallas_call(
        attend_kernel,
        in_specs=[smem, smem] + [vmem] * 5 + [pl.BlockSpec(memory_space=pl.ANY)] * 2,
        out_specs=[vmem] * 3,
        out_shape=[jax.ShapeDtypeStruct((heads, slots, HD), jnp.float32), half, half],
        scratch_shapes=[
            pltpu.VMEM(key_cache.shape, jnp.bfloat16),
            pltpu.VMEM(value_cache.shape, jnp.bfloat16),
            pltpu.SemaphoreType.DMA((2, slots)),
            pltpu.VMEM((heads, slots, HD), jnp.float32),
            pltpu.VMEM(kv_shape, jnp.float32),
            pltpu.VMEM(kv_shape, jnp.float32),
        ],
        compiler_params=pltpu.CompilerParams(vmem_limit_bytes=VMEM),
        name="attend",
    )(
        side.reshape(1),
        lengths,
        by_head(query),
        by_head(new_key),
        by_head(new_value),
        by_head(residual),
        norm_gain.reshape(heads, 1, HD),
        key_cache,
        value_cache,
    )


def times(rows, weight):
    return lax.dot_general(rows, weight, (((1,), (1,)), ((), ())), preferred_element_type=jnp.float32)


def project_kernel(count, *refs):
    *runs, gate_ref, up_ref, out_ref = refs[-3 - count :]
    units = gate_ref.shape[0]
    rows = jnp.concatenate([run[...] for run in runs], axis=0)
    out_ref[0, :, :units] = times(rows, gate_ref[...]).astype(jnp.bfloat16)
    out_ref[0, :, units:] = times(rows, up_ref[...]).astype(jnp.bfloat16)


def project(found, place, count, runs, gate_weight, up_weight):
    features = runs[0].shape[1]
    size = sum(run.shape[0] for run in runs)
    units = gate_weight.shape[0]
    vmem = pl.BlockSpec(memory_space=pltpu.VMEM)
    earlier = [] if found is None else [found]
    return pl.pallas_call(
        functools.partial(project_kernel, len(runs)),
        grid=(1,),
        in_specs=[pl.BlockSpec(memory_space=pl.ANY) for _ in earlier] + [vmem] * (len(runs) + 2),
        out_specs=pl.BlockSpec((1, size, 2 * units), lambda i: (place, 0, 0)),
        out_shape=jax.ShapeDtypeStruct((count, size, 2 * units), jnp.bfloat16),
        input_output_aliases={0: 0} if earlier else {},
        compiler_params=pltpu.CompilerParams(vmem_limit_bytes=24 * 1024 * 1024),
        cost_estimate=pl.CostEstimate(
            flops=4 * size * units * features, bytes_accessed=4 * units * features, transcendentals=0
        ),
        name="project",
    )(*earlier, *runs, gate_weight, up_weight)


def combine_kernel(side_ref, own, other, hidden_ref):
    units = hidden_ref.shape[-1]
    even = side_ref[0] == 0

    def pick(found, third, second, first):
        return found[ORDER.index(third), STEPS.index(second), first].astype(jnp.float32)

    for third in range(RING):
        for second in range(RING):
            for first in range(RING):
                got = jnp.where(
                    even,
                    pick(other, first, third, second),
                    pick(other, second, first, third),
                )
                both = pick(own, third, second, first) + got
                gate, up = both[:, :units], both[:, units:]
                hidden = gate / (1.0 + jnp.exp(-gate)) * up
                hidden_ref[third, second, first] = hidden.astype(jnp.bfloat16)


def combine(side, *halves):
    rows, both = halves[0].shape[-2:]
    return pl.pallas_call(
        combine_kernel,
        in_specs=[pl.BlockSpec(memory_space=pltpu.SMEM)]
        + [pl.BlockSpec(memory_space=pltpu.VMEM) for _ in halves],
        out_specs=pl.BlockSpec(memory_space=pltpu.VMEM),
        out_shape=jax.ShapeDtypeStruct((RING, RING, RING, rows, both // 2), jnp.bfloat16),
        compiler_params=pltpu.CompilerParams(vmem_limit_bytes=24 * 1024 * 1024),
        name="combine",
    )(side, *halves)


def body(
    query,
    new_key,
    new_value,
    key_cache,
    value_cache,
    lengths,
    residual,
    norm_gain,
    gate_weight,
    up_weight,
    down_weight,
):
    slots, width = residual.shape
    half = gate_weight.shape[0]
    hidden_units = gate_weight.shape[1]
    rows = 2 * slots
    side = lax.axis_index("side")
    even = side == 0
    mid, own, other = attend(
        side, query, new_key, new_value, key_cache, value_cache, lengths, residual, norm_gain
    )
    got = lax.ppermute(other, "side", SWAP)
    pair = jnp.stack([jnp.where(even, own, got), jnp.where(even, got, own)])
    pair = pair.transpose(0, 2, 1, 3).reshape(rows, half)

    near = jnp.concatenate(gather_line(pair, "first"), axis=0)
    after, before = fetch(near, "second", 1), fetch(near, "second", 3)
    cut = near.shape[0] // 2
    relayed = [fetch(after[:cut], "second", 1), fetch(before[cut:], "second", 3)]
    early = jnp.concatenate([near, after, before], axis=0)
    late = jnp.concatenate(relayed, axis=0)
    blocks = gather_ring(early, late, "third")

    weights = gate_weight.T, up_weight.T
    found = None
    for place, third in enumerate(ORDER):
        runs = blocks[third]
        if place == 0:
            runs = [behind(run, blocks[FAR][1]) for run in runs]
        found = project(found, place, RING, runs, *weights)
    halves = [found, lax.ppermute(found, "side", SWAP)]
    hidden = combine(
        side.reshape(1), *[h.reshape(-1, RING, RING, rows, 2 * hidden_units) for h in halves]
    )

    cut = RING * RING * rows // 2
    runs = [hidden[third].reshape(2, cut, hidden_units) for third in range(RING)]

    def down(run):
        return dot(run.reshape(-1, hidden_units), down_weight).astype(jnp.bfloat16)

    part_far = down(runs[FAR])
    after, before = send(part_far[:cut], "third", 1), send(part_far[cut:], "third", 3)
    one_bottom = send(down(behind(runs[1][1], part_far)), "third", 1)
    three_top = send(down(behind(runs[3][0], part_far)), "third", 3)
    one_top = down(behind(runs[1][0], part_far))
    three_bottom = down(behind(runs[3][1], part_far))
    part_own = down(behind(runs[0], part_far))
    one_top = send(add(one_top, after), "third", 1)
    three_bottom = send(add(three_bottom, before), "third", 3)
    summed = [
        add(part_own[:cut], one_top, three_top),
        add(part_own[cut:], one_bottom, three_bottom),
    ]
    summed = [run for part in summed for run in (part[: cut // 2], part[cut // 2 :])]
    summed = reduce_line(summed, "second")
    summed = reduce_line(parts(summed), "first")

    by_side = summed.reshape(2, slots, half)
    kept = lax.dynamic_index_in_dim(by_side, side, 0, keepdims=False)
    got = lax.ppermute(lax.dynamic_index_in_dim(by_side, 1 - side, 0, keepdims=False), "side", SWAP)
    ffn = jnp.concatenate([jnp.where(even, kept, got), jnp.where(even, got, kept)], axis=1)
    mid = mid.transpose(1, 0, 2).reshape(slots, width)
    return (mid + ffn.astype(jnp.float32)).astype(jnp.bfloat16)


def solution(mesh):
    in_specs = (
        P(("side", "gx"), None),
        P(("side", "gx"), None),
        P(("side", "gx"), None),
        P(("side", "gx"), None, None),
        P(("side", "gx"), None, None),
        P(("side", "gx")),
        P(("side", "gx"), None),
        P(),
        P("side", "gx"),
        P("side", "gx"),
        P("gx", "side"),
    )
    out_specs = P(("side", "gx"), None)
    return jax.shard_map(body, mesh=mesh, in_specs=in_specs, out_specs=out_specs, check_vma=False)
```

```python
import functools

import jax
import jax.numpy as jnp
from jax import lax
from jax.experimental import pallas as pl
from jax.experimental.pallas import tpu as pltpu
from jax.sharding import PartitionSpec as P

HD = 128
SWAP = [(0, 1), (1, 0)]
RING = 4
VMEM = 60 * 1024 * 1024
TOGETHER = 4
FAR = 2
ORDER = (0, 1, 3, 2)
STEPS = (0, 1, 3, 2)
FAR = 2
PLACE = {(0, 0): (0, 0), (0, 1): (0, 1), (1, 0): (1, 0), (3, 1): (1, 1), (1, 1): (2, 0), (3, 0): (2, 1)}
LINES = {"first": ("x", "z"), "second": ("z", "y"), "third": ("y", "x")}


def chip(z, x, y):
    return (z % RING) * RING * RING + (x % RING) * RING + y % RING


def hops(line, distance):
    pairs = []
    for side in range(2):
        dz, dx, dy = (distance * (axis == LINES[line][side]) for axis in "zxy")
        for z in range(RING):
            for x in range(RING):
                for y in range(RING):
                    here, there = chip(z, x, y), chip(z + dz, x + dx, y + dy)
                    pairs.append((side * RING**3 + here, side * RING**3 + there))
    return pairs


def send(array, line, distance):
    return lax.ppermute(array, ("side", "gx"), hops(line, distance))


def fetch(array, line, distance):
    return lax.ppermute(array, ("side", "gx"), [(there, here) for here, there in hops(line, distance)])


def gather_line(array, line):
    far = fetch(array, line, 2)
    return [array, fetch(array, line, 1), far, fetch(array, line, 3)]


def gather_ring(early, late, line):
    step = late.shape[0]
    after, before = fetch(early, line, 1), fetch(early, line, 3)
    after_late, before_late = fetch(late, line, 1), fetch(late, line, 3)
    far = [
        fetch(after[: 2 * step], line, 1),
        fetch(before[2 * step :], line, 3),
        fetch(behind(before_late, after_late), line, 3),
    ]
    return [[early, late], [after, after_late], far, [before, before_late]]


def behind(array, *others):
    return lax.optimization_barrier((array, *others))[0]


def add(*arrays):
    return sum(array.astype(jnp.float32) for array in arrays).astype(jnp.bfloat16)


def reduce_line(blocks, line):
    far = send(blocks[2], line, 2)
    return add(blocks[0], send(blocks[1], line, 1), far, send(blocks[3], line, 3))


def parts(array):
    rows = array.shape[0] // RING
    return [array[i * rows : (i + 1) * rows] for i in range(RING)]


def dot(left, right):
    return jnp.dot(left, right, preferred_element_type=jnp.float32)


def attend_kernel(
    side_ref, lengths_ref, query_ref, new_key_ref, new_value_ref, residual_ref, gain_ref,
    key_cache, value_cache, mid_ref, own_ref, other_ref,
    key_ref, value_ref, copied, queries, keys_now, values_now,
):
    heads, slots, _ = query_ref.shape
    kv_heads = new_key_ref.shape[0]
    groups = heads // kv_heads
    ctx = key_ref.shape[1]
    scale = 1.0 / HD**0.5
    runs = [range(start, min(start + TOGETHER, slots)) for start in range(0, slots, TOGETHER)]

    def copy(kind, slot):
        cache, held = ((key_cache, key_ref), (value_cache, value_ref))[kind]
        return pltpu.make_async_copy(cache.at[slot], held.at[slot], copied.at[kind, slot])

    for run in runs:
        for kind in range(2):
            for slot in run:
                copy(kind, slot).start()
    queries[...] = query_ref[...].astype(jnp.float32)
    keys_now[...] = new_key_ref[...].astype(jnp.float32)
    values_now[...] = new_value_ref[...].astype(jnp.float32)

    def spread_heads(rows):
        return jnp.broadcast_to(rows[:, None, :], (kv_heads, groups, HD)).reshape(heads, HD)

    row_group = lax.broadcasted_iota(jnp.int32, (heads, kv_heads * HD), 0) // groups
    col_group = lax.broadcasted_iota(jnp.int32, (heads, kv_heads * HD), 1) // HD
    own = row_group == col_group
    places = lax.broadcasted_iota(jnp.int32, (heads, ctx), 1)
    for run in runs:
        query_of, scores_of, probs_of, new_of, total_of = {}, {}, {}, {}, {}
        for slot in run:
            copy(0, slot).wait()
        for slot in run:
            query_of[slot] = queries[:, slot, :]
            wide = jnp.where(own, jnp.concatenate([query_of[slot]] * kv_heads, axis=1), 0)
            scores_of[slot] = lax.dot_general(
                wide.astype(jnp.bfloat16),
                key_ref[slot],
                (((1,), (1,)), ((), ())),
                preferred_element_type=jnp.float32,
            )
        for slot in run:
            scores = jnp.where(places < lengths_ref[slot], scores_of[slot] * scale, -jnp.inf)
            key_now = spread_heads(keys_now[:, slot, :])
            score_new = jnp.sum(query_of[slot] * key_now, axis=1, keepdims=True) * scale
            peak = jnp.maximum(jnp.max(scores, axis=1, keepdims=True), score_new)
            probs = jnp.exp(scores - peak)
            prob_new = jnp.exp(score_new - peak)
            total_of[slot] = jnp.sum(probs, axis=1, keepdims=True) + prob_new
            probs_of[slot] = probs.astype(jnp.bfloat16)
            new_of[slot] = prob_new.astype(jnp.bfloat16).astype(jnp.float32)
        for slot in run:
            copy(1, slot).wait()
        for slot in run:
            value_now = spread_heads(values_now[:, slot, :])
            spread = jnp.dot(probs_of[slot], value_ref[slot], preferred_element_type=jnp.float32)
            picked = jnp.concatenate(
                [
                    spread[g * groups : (g + 1) * groups, g * HD : (g + 1) * HD]
                    for g in range(kv_heads)
                ],
                axis=0,
            )
            summed = picked + new_of[slot] * value_now
            mid_ref[:, slot, :] = summed / total_of[slot]

    mid = residual_ref[...] + mid_ref[...]
    mid_ref[...] = mid
    squares = jnp.sum(jnp.sum(mid * mid, axis=0, keepdims=True), axis=2, keepdims=True)
    mean_sq = squares / (heads * HD)
    normed = (mid * lax.rsqrt(mean_sq + 1e-05) * gain_ref[...]).astype(jnp.bfloat16)
    halves = normed[: heads // 2], normed[heads // 2 :]
    even = side_ref[0] == 0
    own_ref[...] = jnp.where(even, halves[0], halves[1])
    other_ref[...] = jnp.where(even, halves[1], halves[0])


def attend(side, query, new_key, new_value, key_cache, value_cache, lengths, residual, norm_gain):
    slots, width = query.shape
    heads = width // HD

    def by_head(array):
        return array.reshape(slots, -1, HD).transpose(1, 0, 2)

    smem, vmem = (pl.BlockSpec(memory_space=space) for space in (pltpu.SMEM, pltpu.VMEM))
    kv_shape = (new_key.shape[1] // HD, slots, HD)
    half = jax.ShapeDtypeStruct((heads // 2, slots, HD), jnp.bfloat16)
    return pl.pallas_call(
        attend_kernel,
        in_specs=[smem, smem] + [vmem] * 5 + [pl.BlockSpec(memory_space=pl.ANY)] * 2,
        out_specs=[vmem] * 3,
        out_shape=[jax.ShapeDtypeStruct((heads, slots, HD), jnp.float32), half, half],
        scratch_shapes=[
            pltpu.VMEM(key_cache.shape, jnp.bfloat16),
            pltpu.VMEM(value_cache.shape, jnp.bfloat16),
            pltpu.SemaphoreType.DMA((2, slots)),
            pltpu.VMEM((heads, slots, HD), jnp.float32),
            pltpu.VMEM(kv_shape, jnp.float32),
            pltpu.VMEM(kv_shape, jnp.float32),
        ],
        compiler_params=pltpu.CompilerParams(vmem_limit_bytes=VMEM),
        name="attend",
    )(
        side.reshape(1),
        lengths,
        by_head(query),
        by_head(new_key),
        by_head(new_value),
        by_head(residual),
        norm_gain.reshape(heads, 1, HD),
        key_cache,
        value_cache,
    )


def times(rows, weight):
    return lax.dot_general(rows, weight, (((1,), (1,)), ((), ())), preferred_element_type=jnp.float32)


def project_kernel(count, *refs):
    *runs, gate_ref, up_ref, out_ref = refs[-3 - count :]
    units = gate_ref.shape[0]
    rows = jnp.concatenate([run[...] for run in runs], axis=0)
    out_ref[0, :, :units] = times(rows, gate_ref[...]).astype(jnp.bfloat16)
    out_ref[0, :, units:] = times(rows, up_ref[...]).astype(jnp.bfloat16)


def project(found, place, count, runs, gate_weight, up_weight):
    features = runs[0].shape[1]
    size = sum(run.shape[0] for run in runs)
    units = gate_weight.shape[0]
    vmem = pl.BlockSpec(memory_space=pltpu.VMEM)
    earlier = [] if found is None else [found]
    return pl.pallas_call(
        functools.partial(project_kernel, len(runs)),
        grid=(1,),
        in_specs=[pl.BlockSpec(memory_space=pl.ANY) for _ in earlier] + [vmem] * (len(runs) + 2),
        out_specs=pl.BlockSpec((1, size, 2 * units), lambda i: (place, 0, 0)),
        out_shape=jax.ShapeDtypeStruct((count, size, 2 * units), jnp.bfloat16),
        input_output_aliases={0: 0} if earlier else {},
        compiler_params=pltpu.CompilerParams(vmem_limit_bytes=24 * 1024 * 1024),
        cost_estimate=pl.CostEstimate(
            flops=4 * size * units * features, bytes_accessed=4 * units * features, transcendentals=0
        ),
        name="project",
    )(*earlier, *runs, gate_weight, up_weight)


def combine_kernel(side_ref, own, other, hidden_ref):
    units = hidden_ref.shape[-1]
    even = side_ref[0] == 0

    def pick(found, third, second, first):
        return found[ORDER.index(third), STEPS.index(second), first].astype(jnp.float32)

    for third in range(RING):
        for second in range(RING):
            for first in range(RING):
                got = jnp.where(
                    even,
                    pick(other, first, third, second),
                    pick(other, second, first, third),
                )
                both = pick(own, third, second, first) + got
                gate, up = both[:, :units], both[:, units:]
                hidden = gate / (1.0 + jnp.exp(-gate)) * up
                hidden_ref[third, second, first] = hidden.astype(jnp.bfloat16)


def combine(side, *halves):
    rows, both = halves[0].shape[-2:]
    return pl.pallas_call(
        combine_kernel,
        in_specs=[pl.BlockSpec(memory_space=pltpu.SMEM)]
        + [pl.BlockSpec(memory_space=pltpu.VMEM) for _ in halves],
        out_specs=pl.BlockSpec(memory_space=pltpu.VMEM),
        out_shape=jax.ShapeDtypeStruct((RING, RING, RING, rows, both // 2), jnp.bfloat16),
        compiler_params=pltpu.CompilerParams(vmem_limit_bytes=24 * 1024 * 1024),
        name="combine",
    )(side, *halves)


def body(
    query,
    new_key,
    new_value,
    key_cache,
    value_cache,
    lengths,
    residual,
    norm_gain,
    gate_weight,
    up_weight,
    down_weight,
):
    slots, width = residual.shape
    half = gate_weight.shape[0]
    hidden_units = gate_weight.shape[1]
    rows = 2 * slots
    side = lax.axis_index("side")
    even = side == 0
    mid, own, other = attend(
        side, query, new_key, new_value, key_cache, value_cache, lengths, residual, norm_gain
    )
    got = lax.ppermute(other, "side", SWAP)
    pair = jnp.stack([jnp.where(even, own, got), jnp.where(even, got, own)])
    pair = pair.transpose(0, 2, 1, 3).reshape(rows, half)

    near = jnp.concatenate(gather_line(pair, "first"), axis=0)
    after, before = fetch(near, "second", 1), fetch(near, "second", 3)
    cut = near.shape[0] // 2
    relayed = [fetch(after[:cut], "second", 1), fetch(before[cut:], "second", 3)]
    early = jnp.concatenate([near, after, before], axis=0)
    late = jnp.concatenate(relayed, axis=0)
    blocks = gather_ring(early, late, "third")

    weights = gate_weight.T, up_weight.T
    found = None
    for place, third in enumerate(ORDER):
        runs = blocks[third]
        if place == 1:
            runs = [behind(run, blocks[FAR][1]) for run in runs]
        found = project(found, place, RING, runs, *weights)
    halves = [found, lax.ppermute(found, "side", SWAP)]
    hidden = combine(
        side.reshape(1), *[h.reshape(-1, RING, RING, rows, 2 * hidden_units) for h in halves]
    )

    cut = RING * RING * rows // 2
    runs = [hidden[third].reshape(2, cut, hidden_units) for third in range(RING)]

    def down(run):
        return dot(run.reshape(-1, hidden_units), down_weight).astype(jnp.bfloat16)

    part_far = down(runs[FAR])
    after, before = send(part_far[:cut], "third", 1), send(part_far[cut:], "third", 3)
    one_bottom = send(down(behind(runs[1][1], part_far)), "third", 1)
    three_top = send(down(behind(runs[3][0], part_far)), "third", 3)
    one_top = down(behind(runs[1][0], part_far))
    three_bottom = down(behind(runs[3][1], part_far))
    part_own = down(behind(runs[0], part_far))
    one_top = send(add(one_top, after), "third", 1)
    three_bottom = send(add(three_bottom, before), "third", 3)
    summed = [
        add(part_own[:cut], one_top, three_top),
        add(part_own[cut:], one_bottom, three_bottom),
    ]
    summed = [run for part in summed for run in (part[: cut // 2], part[cut // 2 :])]
    summed = reduce_line(summed, "second")
    summed = reduce_line(parts(summed), "first")

    by_side = summed.reshape(2, slots, half)
    kept = lax.dynamic_index_in_dim(by_side, side, 0, keepdims=False)
    got = lax.ppermute(lax.dynamic_index_in_dim(by_side, 1 - side, 0, keepdims=False), "side", SWAP)
    ffn = jnp.concatenate([jnp.where(even, kept, got), jnp.where(even, got, kept)], axis=1)
    mid = mid.transpose(1, 0, 2).reshape(slots, width)
    return (mid + ffn.astype(jnp.float32)).astype(jnp.bfloat16)


def solution(mesh):
    in_specs = (
        P(("side", "gx"), None),
        P(("side", "gx"), None),
        P(("side", "gx"), None),
        P(("side", "gx"), None, None),
        P(("side", "gx"), None, None),
        P(("side", "gx")),
        P(("side", "gx"), None),
        P(),
        P("side", "gx"),
        P("side", "gx"),
        P("gx", "side"),
    )
    out_specs = P(("side", "gx"), None)
    return jax.shard_map(body, mesh=mesh, in_specs=in_specs, out_specs=out_specs, check_vma=False)
```
